32 devices in a mesh: lev: 8 (over y, x, core), lat: 4 (over z).
Axes of the slice: x: 2, y: 2, z: 4, core: 2. Of those that a mesh axis runs over, the one named last changes fastest.
Arguments:
- adjoint_in: float32 [8, 64, 16, 2048], P(None, 'lev', 'lat'), may hold values from -6 to 6
- courant_lon: float32 [64, 16, 2048], P('lev', 'lat'), may hold values from -0.24 to 0.24
- courant_lat: float32 [64, 16, 2048], P('lev', 'lat'), may hold values from -0.24 to 0.24, as said below
- mass_flux: float32 [16, 2048], P('lat'), may hold values from 0.1 to 0.9
- conv_band: int32 [2, 16, 2048], P(None, 'lat'), may hold values from 24 to 64, as said below
- diff_inverse: float32 [16, 4, 16, 16], P('lat'), may hold values from 0 to 1
- obs_values: float32 [8, 4, 4, 16, 64], P('lev', 'lat'), may hold values from -6 to 6
- obs_column: int32 [8, 4, 4, 16], P('lev', 'lat'), may hold values from 0 to 1023
- obs_count: int32 [8, 4, 4], P('lev', 'lat'), may hold values from 0 to 16, as said below
Outputs:
- adjoint_out: float32 [8, 64, 16, 2048], P(None, 'lev', 'lat')
The draws below stay inside these ranges and needn't reach their ends.
Inputs may be any that keep to these rules, and one draw needn't show every extreme that they name: `courant_lat`: the south face of the first latitude row carries no flow. `conv_band`: bands hold 4 to 32 levels. `obs_count`: slots at and after the count hold padding. `obs_column`: several soundings may share a column.
All inputs are finite; a program needn't handle non-finite values.
Results may differ from the reference program's by a relative error of at most 0.00007.
Values sent between devices are 32-bit elements; how exact they have to be, the bound alone decides.
A program may use at most 128 MiB of HBM per device.

```python
import math
import jax
import jax.numpy as jnp
from jax import lax

TRACERS = 8
LEVELS = 64
BLK = 16
NB = 4
LAT_DEV = 4
LAT = 16
LON = 2048
COLS_BLOCK = 1024
CAP = 16
ADV_STEPS = 2
N_LEV = 8
N_LAT = 4


def draw_courant_lat(key, part):
    shape = (LEVELS, LAT, LON)
    values = jax.random.uniform(key, shape, jnp.float32, -0.24, 0.24)
    rows = lax.broadcasted_iota(jnp.int32, shape, 1)
    return jnp.where(rows > 0, values, jnp.float32(0.0))


def draw_conv_band(key, part):
    first_key, second_key = jax.random.split(jax.random.fold_in(key, 11))
    upper = jax.random.randint(first_key, (LAT, LON), LEVELS - LEVELS // 8, LEVELS + 1)
    length = jax.random.randint(second_key, (LAT, LON), 4, LEVELS // 2 + 1)
    return jnp.stack([upper - length, upper]).astype(jnp.int32)


def draw_diff_inverse(key, part):
    shape = (LAT, NB, BLK, BLK)
    first_key, second_key = jax.random.split(jax.random.fold_in(key, 23))
    diagonal = jax.random.uniform(first_key, shape, jnp.float32, 0.5, 1.0)
    off_top = 0.6 / (BLK - 1)
    off_diagonal = jax.random.uniform(second_key, shape, jnp.float32, 0.0, off_top)
    is_diagonal = lax.broadcasted_iota(jnp.int32, shape, 2) == lax.broadcasted_iota(jnp.int32, shape, 3)
    return jnp.where(is_diagonal, diagonal, off_diagonal)


def draw_obs_count(key, part):
    shape = (N_LEV, N_LAT, N_LAT)
    first_key, second_key = jax.random.split(jax.random.fold_in(key, 37))
    counts = jax.random.randint(first_key, shape, 0, CAP + 1)
    busiest = jax.random.randint(second_key, (N_LEV, 1, 1), 0, N_LAT)
    destination = lax.broadcasted_iota(jnp.int32, shape, 2)
    return jnp.where(destination == busiest, CAP, counts).astype(jnp.int32)


def set_ends(entries, own_key, smallest, top_value):
    dims = entries.shape
    index_at = [jax.random.randint(jax.random.fold_in(own_key, axis), (), 0, dims[axis]) for axis in range(len(dims))]
    entries = entries.at[tuple(index_at)].set(smallest)
    longest = dims.index(max(dims))
    index_at[longest] = (index_at[longest] + 1) % dims[longest]
    return entries.at[tuple(index_at)].set(top_value)


def steps_of(rng, dims, pieces, low, largest):
    level, own = 1.0, jax.random.fold_in(rng, 6)
    for dim, blocks in pieces:
        heights = jnp.exp(jax.random.uniform(jax.random.fold_in(own, dim), (blocks,), jnp.float32, low / len(pieces), largest / len(pieces)))
        level = level * jnp.repeat(heights, dims[dim] // blocks).reshape([-1 if axis == dim else 1 for axis in range(len(dims))])
    return level


def centred(rng, dims, width, reach, pieces=(), kind=jnp.bfloat16):
    entries = width * jax.random.normal(rng, dims, jnp.float32)
    if pieces:
        entries = entries * steps_of(rng, dims, pieces, -0.22, 0.18)
    return jnp.clip(entries, -reach, reach).astype(kind)


def setup_inputs(seed: int = 0) -> dict:
    keys = jax.random.split(jax.random.key(seed), 10)
    adjoint_in = centred(keys[0], (TRACERS, LEVELS, LAT, LON), 1.0, 6.0, ((1, 8), (2, 4)), jnp.float32)
    courant_lon = jnp.clip(jax.random.uniform(keys[1], (LEVELS, LAT, LON), jnp.float32, -0.24, 0.24) * steps_of(keys[1], (LEVELS, LAT, LON), ((0, 8), (1, 4)), -0.4, 0.0), -0.24, 0.24)
    courant_lat = draw_courant_lat(jax.random.fold_in(keys[9], 71), 0)
    mass_flux = jnp.clip(jnp.exp(math.log(0.9) - 2.1972245 * jax.random.uniform(keys[3], (LAT, LON), jnp.float32) ** steps_of(keys[3], (LAT, LON), ((0, 4),), -0.2, 0.2)), 0.1, 0.9)
    conv_band = draw_conv_band(jax.random.fold_in(keys[9], 71), 0)
    diff_inverse = draw_diff_inverse(jax.random.fold_in(keys[9], 71), 0)
    obs_values = centred(keys[6], (N_LEV, N_LAT, N_LAT, CAP, LEVELS), 1.0, 6.0, ((0, 8), (1, 4)), jnp.float32)
    obs_column = set_ends(jax.random.randint(keys[7], (N_LEV, N_LAT, N_LAT, CAP), 0, COLS_BLOCK), jax.random.fold_in(keys[7], 1), 0, COLS_BLOCK - 1).astype(jnp.int32)
    obs_count = draw_obs_count(jax.random.fold_in(keys[9], 71), 0)
    return {"adjoint_in": adjoint_in, "courant_lon": courant_lon, "courant_lat": courant_lat, "mass_flux": mass_flux, "conv_band": conv_band, "diff_inverse": diff_inverse, "obs_values": obs_values, "obs_column": obs_column, "obs_count": obs_count}


def advect(padded_rows, lat_faces, lon_faces):
    row_total = lon_faces.shape[-2]
    center_rows = padded_rows[..., 1:row_total + 1, :]
    northern = padded_rows[..., 2:row_total + 2, :]
    southern = padded_rows[..., 0:row_total, :]
    face_south = lat_faces[..., 0:row_total, :]
    face_north = lat_faces[..., 1:row_total + 1, :]
    face_east = jnp.roll(lon_faces, -1, axis=-1)
    eastern = jnp.roll(center_rows, -1, axis=-1)
    western = jnp.roll(center_rows, 1, axis=-1)
    flow_east = jnp.maximum(face_east, 0.0)
    flow_west = jnp.minimum(lon_faces, 0.0)
    flow_north = jnp.maximum(face_north, 0.0)
    flow_south = jnp.minimum(face_south, 0.0)
    center = 1.0 - flow_east + flow_west - flow_north + flow_south
    return center_rows * center + eastern * flow_east - western * flow_west + northern * flow_north - southern * flow_south


def reference(adjoint_in, courant_lon, courant_lat, mass_flux, conv_band, diff_inverse, obs_values, obs_column, obs_count):
    state = adjoint_in
    lat_padded = jnp.concatenate([courant_lat, jnp.zeros_like(courant_lat[:, :1])], axis=1)
    for substep in range(ADV_STEPS):
        padded = jnp.pad(state, ((0, 0), (0, 0), (1, 1), (0, 0)))
        state = advect(padded, lat_padded, courant_lon)
    levels = jnp.arange(LEVELS, dtype=jnp.int32)[:, None, None]
    inside = ((levels >= conv_band[0][None]) & (levels < conv_band[1][None])).astype(jnp.float32)
    counted = (conv_band[1] - conv_band[0]).astype(jnp.float32)
    band_mean = jnp.sum(state * inside[None], axis=1) / counted
    state = state + mass_flux * inside[None] * (band_mean[:, None] - state)
    blocked = state.reshape(TRACERS, NB, BLK, LAT, LON)
    state = jnp.einsum("rbij,tbjrl->tbirl", diff_inverse, blocked, precision=lax.Precision.HIGHEST).reshape(TRACERS, LEVELS, LAT, LON)
    slot_ids = jnp.arange(CAP, dtype=jnp.int32)
    valid_slot = slot_ids[None, None, None, :] < obs_count[..., None]
    holder_lev = jnp.arange(N_LEV, dtype=jnp.int32)[:, None, None, None]
    dest_group = jnp.arange(N_LAT, dtype=jnp.int32)[None, None, :, None]
    target = (dest_group * (LAT_DEV * LON) + holder_lev * COLS_BLOCK + obs_column).astype(jnp.int32)
    weighted = jnp.where(valid_slot[..., None], obs_values, jnp.float32(0.0))
    forcing = jax.ops.segment_sum(weighted.reshape(-1, LEVELS), target.reshape(-1), num_segments=LAT * LON)
    forcing = forcing.T.reshape(LEVELS, LAT, LON)
    return state + forcing[None]
```

```python
import functools

import jax
import jax.numpy as jnp
from jax import lax
from jax.experimental import pallas as pl
from jax.experimental.pallas import tpu as pltpu
from jax.sharding import PartitionSpec as P

MESH = pl.DeviceIdType.MESH
LANES = 128


def kernel(
    lev_n, lat_n,
    a_ref, u_ref, v_ref, band_ref, flux_ref, diff_ref, obs_ref,
    out_ref,
    a1, a2, a2o, halo0, halo1, vnorth, cc, fe, fw, fn, fs,
    io, ip, go, gp, mx, bs, bsr, bmean, force, obs_in, msg, got,
    s_obs1, r_obs1, s_obs2, r_obs2, s_v, r_v, s_h0, r_h0, s_h1, r_h1, s_pair, r_pair, s_bs, r_bs,
):
    T, R, C, L, _ = a_ref.shape
    lev = lax.axis_index("lev")
    lat = lax.axis_index("lat")
    chips = lev_n // 2
    partner = lev + 1 - 2 * (lev % 2)
    has_north = lat < lat_n - 1
    has_south = lat > 0
    tiles = R * C // lev_n
    levels = lev_n * L

    def remote(src, dst, s, r, dev):
        return pltpu.make_async_remote_copy(
            src_ref=src, dst_ref=dst, send_sem=s, recv_sem=r, device_id=dev, device_id_type=MESH
        )

    def obs1(d):
        to = (lat + d) % lat_n
        return remote(obs_ref.at[to], obs_in.at[d - 1], s_obs1.at[d - 1], r_obs1.at[d - 1], (lev, to))

    def obs2(d):
        to = (lev + d) % lev_n
        return remote(msg.at[to], got.at[lev], s_obs2.at[d - 1], r_obs2.at[d - 1], (to, lat))

    def obs2_wait(d):
        src = (lev - d + lev_n) % lev_n
        return remote(msg.at[src], got.at[src], s_obs2.at[d - 1], r_obs2.at[d - 1], (src, lat))

    def south(src, dst, s, r):
        return remote(src, dst, s, r, (lev, lax.max(lat - 1, 0)))

    def north(src, dst, s, r):
        return remote(src, dst, s, r, (lev, lax.min(lat + 1, lat_n - 1)))

    def v_copy():
        return south(v_ref.at[0], vnorth, s_v, r_v)

    def halo_south(src, dst, s, r, t):
        return south(src.at[t, 0], dst.at[1, t], s.at[1, t], r.at[1, t])

    def halo_north(src, dst, s, r, t):
        return north(src.at[t, R - 1], dst.at[0, t], s.at[0, t], r.at[0, t])

    def halo_send(src, dst, s, r, t):
        @pl.when(has_south)
        def _():
            halo_south(src, dst, s, r, t).start()

        @pl.when(has_north)
        def _():
            halo_north(src, dst, s, r, t).start()

    def halo_recv(src, dst, s, r, t):
        @pl.when(has_south)
        def _():
            halo_north(src, dst, s, r, t).wait_recv()

        @pl.when(has_north)
        def _():
            halo_south(src, dst, s, r, t).wait_recv()

    def halo_sent(src, dst, s, r, t):
        @pl.when(has_south)
        def _():
            halo_south(src, dst, s, r, t).wait_send()

        @pl.when(has_north)
        def _():
            halo_north(src, dst, s, r, t).wait_send()

    def pair(t):
        return remote(a2.at[t], a2o.at[t], s_pair.at[t], r_pair.at[t], (partner, lat))

    def sums(d, t):
        to = (lev + 2 * d) % lev_n
        return remote(bs.at[t], bsr.at[d - 1, t], s_bs.at[d - 1, t], r_bs.at[d - 1, t], (to, lat))

    barrier = pltpu.get_barrier_semaphore()
    for d in range(1, lat_n):
        pl.semaphore_signal(barrier, inc=1, device_id=(lev, (lat + d) % lat_n), device_id_type=MESH)
    for d in range(1, lev_n):
        pl.semaphore_signal(barrier, inc=1, device_id=((lev + d) % lev_n, lat), device_id_type=MESH)
    pl.semaphore_wait(barrier, lat_n + lev_n - 2)

    for d in range(1, lat_n):
        obs1(d).start()

    @pl.when(has_south)
    def _():
        v_copy().start()

    @pl.loop(0, T)
    def _(t):
        halo_send(a_ref, halo0, s_h0, r_h0, t)

    @pl.when(jnp.logical_not(has_south))
    def _():
        halo0[0] = jnp.zeros_like(halo0[0])
        halo1[0] = jnp.zeros_like(halo1[0])

    @pl.when(jnp.logical_not(has_north))
    def _():
        halo0[1] = jnp.zeros_like(halo0[1])
        halo1[1] = jnp.zeros_like(halo1[1])
        vnorth[...] = jnp.zeros_like(vnorth)

    lane = lax.broadcasted_iota(jnp.int32, (C, L, LANES), 2)

    def eastern(x):
        r = pltpu.roll(x, LANES - 1, 2)
        return jnp.where(lane == LANES - 1, jnp.concatenate([r[1:], r[:1]], axis=0), r)

    def western(x):
        r = pltpu.roll(x, 1, 2)
        return jnp.where(lane == 0, jnp.concatenate([r[-1:], r[:-1]], axis=0), r)

    level = lax.broadcasted_iota(jnp.int32, (L, LANES), 0)
    for r in range(R):
        for c in range(C):
            k = r * C + c
            lo = jnp.broadcast_to(band_ref[0, k : k + 1, :], (L, LANES))
            hi = jnp.broadcast_to(band_ref[1, k : k + 1, :], (L, LANES))
            kap = jnp.broadcast_to(flux_ref[k : k + 1, :], (L, LANES))
            for base, inside, g in ((lev * L, io, go), (partner * L, ip, gp)):
                here = jnp.where(level + base >= lo, 1.0, 0.0) * jnp.where(level + base < hi, 1.0, 0.0)
                inside[r, c] = here
                g[r, c] = kap * here

    @pl.when(has_north)
    def _():
        v_copy().wait_recv()

    for r in range(R):
        u = u_ref[r]
        e = jnp.maximum(eastern(u), 0.0)
        w = jnp.minimum(u, 0.0)
        n = jnp.maximum(v_ref[r + 1] if r < R - 1 else vnorth[...], 0.0)
        s = jnp.minimum(v_ref[r], 0.0)
        fe[r], fw[r], fn[r], fs[r] = e, w, n, s
        cc[r] = 1.0 - e + w - n + s

    def substep(src, halo, dst, t):
        for r in range(R):
            x = src[t, r]
            up = src[t, r + 1] if r < R - 1 else halo[1, t]
            down = src[t, r - 1] if r > 0 else halo[0, t]
            dst[t, r] = (
                x * cc[r] + eastern(x) * fe[r] - western(x) * fw[r] + up * fn[r] - down * fs[r]
            )

    for d in range(1, lat_n):
        obs1(d).wait_recv()
    total = obs_ref[lat]
    for d in range(1, lat_n):
        total = total + obs_in[d - 1]
    for i in range(lev_n):
        msg[i, 0:L] = total[i * L : (i + 1) * L]
        msg[i, L : 2 * L] = total[levels : levels + L]
    got[lev] = msg[lev]
    for d in range(1, lev_n):
        obs2(d).start()

    @pl.loop(0, T)
    def _(t):
        halo_recv(a_ref, halo0, s_h0, r_h0, t)
        substep(a_ref, halo0, a1, t)
        halo_send(a1, halo1, s_h1, r_h1, t)

    for d in range(1, lev_n):
        obs2_wait(d).wait_recv()
    width = got.shape[2]
    diagonal = lax.broadcasted_iota(jnp.int32, (width, width), 0) == lax.broadcasted_iota(
        jnp.int32, (width, width), 1
    )

    @pl.loop(0, lev_n)
    def _(i):
        values = got[i, 0:L]
        row = got[i, L : 2 * L][0:1]
        column = jnp.sum(jnp.where(diagonal, jnp.broadcast_to(row, (width, width)), 0.0), axis=1, keepdims=True)
        column = column.astype(jnp.int32) - 1
        high = values.astype(jnp.bfloat16).astype(jnp.float32)
        rest = values - high
        middle = rest.astype(jnp.bfloat16).astype(jnp.float32)
        parts = jnp.concatenate([high, middle, rest - middle, jnp.zeros_like(high)], axis=0).astype(jnp.bfloat16)
        for c in range(tiles):
            ids = lax.broadcasted_iota(jnp.int32, (width, LANES), 1) + c * LANES
            hot = jnp.where(column == ids, 1.0, 0.0).astype(jnp.bfloat16)
            f = jnp.dot(parts, hot, preferred_element_type=jnp.float32)
            force[i * tiles + c] = f[0:L] + f[L : 2 * L] + f[2 * L : 3 * L]

    counted = (band_ref[1] - band_ref[0]).astype(jnp.float32)

    def stage_a(t):
        halo_recv(a1, halo1, s_h1, r_h1, t)
        substep(a1, halo1, a2, t)
        pair(t).start()

    def stage_b(t):
        pair(t).wait_recv()
        for r in range(R):
            x = a2[t, r] * io[r] + a2o[t, r] * ip[r]
            bs[t, r * C : (r + 1) * C, :] = jnp.sum(x, axis=1)
        for d in range(1, chips):
            sums(d, t).start()

    def stage_c(t):
        acc = bs[t]
        for d in range(1, chips):
            sums(d, t).wait_recv()
            acc = acc + bsr[d - 1, t]
        bmean[...] = acc / counted
        for r in range(R):
            for c in range(C):
                k = r * C + c
                m = jnp.broadcast_to(bmean[k : k + 1, :], (L, LANES))
                x = a2[t, r, c]
                y = a2o[t, r, c]
                mx[r, c, 0:L] = x + go[r, c] * (m - x)
                mx[r, c, L : 2 * L] = y + gp[r, c] * (m - y)
        for r in range(R):
            acc = force[r * C : (r + 1) * C]
            for j in range(2 * L):
                acc = acc + diff_ref[r, j][None] * mx[r, :, j : j + 1, :]
            out_ref[t, r] = acc

    @pl.loop(0, T + 2)
    def _(s):
        @pl.when(s < T)
        def _():
            stage_a(s)

        @pl.when(jnp.logical_and(s >= 1, s < T + 1))
        def _():
            stage_b(s - 1)

        @pl.when(s >= 2)
        def _():
            stage_c(s - 2)

    for d in range(1, lat_n):
        obs1(d).wait_send()
    for d in range(1, lev_n):
        obs2(d).wait_send()

    @pl.when(has_south)
    def _():
        v_copy().wait_send()

    @pl.loop(0, T)
    def _(t):
        halo_sent(a_ref, halo0, s_h0, r_h0, t)
        halo_sent(a1, halo1, s_h1, r_h1, t)
        pair(t).wait_send()
        for d in range(1, chips):
            sums(d, t).wait_send()


def body(
    adjoint_in, courant_lon, courant_lat, mass_flux, conv_band, diff_inverse,
    obs_values, obs_column, obs_count,
):
    lev_n, lat_n = lax.axis_size("lev"), lax.axis_size("lat")
    lev, lat = lax.axis_index("lev"), lax.axis_index("lat")
    T, L, R, lon = adjoint_in.shape
    C = lon // LANES
    K = R * C
    levels, cap = obs_values.shape[-1], obs_values.shape[-2]

    a = adjoint_in.reshape(T, L, R, C, LANES).transpose(0, 2, 3, 1, 4)
    u = courant_lon.reshape(L, R, C, LANES).transpose(1, 2, 0, 3)
    v = courant_lat.reshape(L, R, C, LANES).transpose(1, 2, 0, 3)
    band = conv_band.reshape(2, K, LANES)
    flux = mass_flux.reshape(K, LANES)

    size = diff_inverse.shape[-1]
    block, first = lev * L // size, lev * L % size
    inverse = lax.dynamic_index_in_dim(diff_inverse, block, axis=1, keepdims=False)
    inverse = lax.dynamic_slice_in_dim(inverse, first, L, axis=1)
    inverse = jnp.where(first > 0, jnp.roll(inverse, -L, axis=2), inverse)
    diff = jnp.broadcast_to(inverse.transpose(0, 2, 1)[..., None], (R, size, L, LANES))

    width = -(-lat_n * cap // LANES) * LANES
    slots = lax.broadcasted_iota(jnp.int32, (lat_n, cap), 1)
    column = jnp.where(slots < obs_count[0, 0][:, None], obs_column[0, 0] + 1, 0).astype(jnp.float32)
    rows = jnp.concatenate(
        [obs_values[0, 0].transpose(0, 2, 1), jnp.broadcast_to(column[:, None], (lat_n, L, cap))], axis=1
    )
    obs = lax.dynamic_update_slice(
        jnp.zeros((lat_n, levels + L, width), jnp.float32), rows, (0, 0, lat * cap)
    )

    chips = lev_n // 2
    f32 = jnp.float32
    vm = lambda *shape: pltpu.VMEM(shape, f32)
    dma = lambda *shape: pltpu.SemaphoreType.DMA(shape)
    scratch = [
        vm(T, R, C, L, LANES), vm(T, R, C, L, LANES), vm(T, R, C, L, LANES),
        vm(2, T, C, L, LANES), vm(2, T, C, L, LANES), vm(C, L, LANES),
        *[vm(R, C, L, LANES)] * 9,
        vm(R, C, 2 * L, LANES), vm(T, K, LANES), vm(chips - 1, T, K, LANES), vm(K, LANES),
        vm(K, L, LANES), vm(lat_n - 1, levels + L, width), vm(lev_n, 2 * L, width), vm(lev_n, 2 * L, width),
        dma(lat_n - 1), dma(lat_n - 1), dma(lev_n - 1), dma(lev_n - 1),
        pltpu.SemaphoreType.DMA, pltpu.SemaphoreType.DMA,
        dma(2, T), dma(2, T), dma(2, T), dma(2, T), dma(T), dma(T), dma(chips - 1, T), dma(chips - 1, T),
    ]
    out = pl.pallas_call(
        functools.partial(kernel, lev_n, lat_n),
        out_shape=jax.ShapeDtypeStruct((T, R, C, L, LANES), f32),
        in_specs=[pl.BlockSpec(memory_space=pltpu.VMEM)] * 7,
        out_specs=pl.BlockSpec(memory_space=pltpu.VMEM),
        scratch_shapes=scratch,
        compiler_params=pltpu.CompilerParams(
            collective_id=0, has_side_effects=True, vmem_limit_bytes=44 * 1024 * 1024
        ),
    )(a, u, v, band, flux, diff, obs)
    return out.transpose(0, 3, 1, 2, 4).reshape(T, L, R, lon)


def solution(mesh):
    placed = (
        P(None, "lev", "lat", None),
        P("lev", "lat", None),
        P("lev", "lat", None),
        P("lat", None),
        P(None, "lat", None),
        P("lat", None, None, None),
        P("lev", "lat", None, None, None),
        P("lev", "lat", None, None),
        P("lev", "lat", None),
    )
    return jax.shard_map(
        body, mesh=mesh, in_specs=placed, out_specs=P(None, "lev", "lat", None), check_vma=False
    )
```

```python
import functools

import jax
import jax.numpy as jnp
from jax import lax
from jax.experimental import pallas as pl
from jax.experimental.pallas import tpu as pltpu
from jax.sharding import PartitionSpec as P

MESH = pl.DeviceIdType.MESH
LANES = 128


def kernel(
    lev_n, lat_n,
    raw_a, raw_u, raw_v, band_ref, flux_ref, inv_ref, values_ref, column_ref, count_ref,
    out_ref,
    stage, stage_u, stage_v, a_ref, u_ref, v_ref, diff_ref, obs_ref, counted,
    a1, a2, a2o, halo0, halo1, vnorth, cc, fe, fw, fn, fs,
    io, go, gp, mx, ps, pr, hs, bsr, bmean, force, obs_in, msg, got,
    c_a, c_u, c_v, s_obs1, r_obs1, s_obs2, r_obs2, s_v, r_v, s_h0, r_h0, s_h1, r_h1, s_pair, r_pair,
    s_part, r_part, s_bs, r_bs, s_mean, r_mean,
):
    T, R, C, L, _ = a_ref.shape
    K = R * C
    H = K // 2
    half = lax.axis_index("lev") % 2
    lev = lax.axis_index("lev")
    lat = lax.axis_index("lat")
    chips = lev_n // 2
    partner = lev + 1 - 2 * (lev % 2)
    has_north = lat < lat_n - 1
    has_south = lat > 0
    tiles = R * C // lev_n
    levels = lev_n * L
    cap = values_ref.shape[3]
    first = pl.multiple_of(half * L, L)
    mine = pl.ds(pl.multiple_of(half * H, H), H)
    other = pl.ds(pl.multiple_of((1 - half) * H, H), H)

    def remote(src, dst, s, r, dev):
        return pltpu.make_async_remote_copy(
            src_ref=src, dst_ref=dst, send_sem=s, recv_sem=r, device_id=dev, device_id_type=MESH
        )

    def obs1(d):
        to = (lat + d) % lat_n
        return remote(obs_ref.at[to], obs_in.at[pl.ds(d * cap, cap)], s_obs1.at[d - 1], r_obs1.at[d - 1], (lev, to))

    def obs2(d):
        to = (lev + d) % lev_n
        return remote(msg.at[to], got.at[lev], s_obs2.at[d - 1], r_obs2.at[d - 1], (to, lat))

    def obs2_wait(d):
        src = (lev - d + lev_n) % lev_n
        return remote(msg.at[src], got.at[src], s_obs2.at[d - 1], r_obs2.at[d - 1], (src, lat))

    def south(src, dst, s, r):
        return remote(src, dst, s, r, (lev, lax.max(lat - 1, 0)))

    def north(src, dst, s, r):
        return remote(src, dst, s, r, (lev, lax.min(lat + 1, lat_n - 1)))

    def v_copy():
        return south(v_ref.at[0], vnorth, s_v, r_v)

    def halo_south(src, dst, s, r, t):
        return south(src.at[t, 0], dst.at[1, t], s.at[1, t], r.at[1, t])

    def halo_north(src, dst, s, r, t):
        return north(src.at[t, R - 1], dst.at[0, t], s.at[0, t], r.at[0, t])

    def halo_send(src, dst, s, r, t):
        @pl.when(has_south)
        def _():
            halo_south(src, dst, s, r, t).start()

        @pl.when(has_north)
        def _():
            halo_north(src, dst, s, r, t).start()

    def halo_recv(src, dst, s, r, t):
        @pl.when(has_south)
        def _():
            halo_north(src, dst, s, r, t).wait_recv()

        @pl.when(has_north)
        def _():
            halo_south(src, dst, s, r, t).wait_recv()

    def halo_sent(src, dst, s, r, t):
        @pl.when(has_south)
        def _():
            halo_south(src, dst, s, r, t).wait_send()

        @pl.when(has_north)
        def _():
            halo_north(src, dst, s, r, t).wait_send()

    def pair(t):
        return remote(a2.at[t], a2o.at[t], s_pair.at[t], r_pair.at[t], (partner, lat))

    def part(t):
        return remote(ps.at[t, other], pr.at[t], s_part.at[t], r_part.at[t], (partner, lat))

    def sums(d, t):
        to = (lev + 2 * d) % lev_n
        return remote(hs.at[t], bsr.at[d - 1, t], s_bs.at[d - 1, t], r_bs.at[d - 1, t], (to, lat))

    def mean(t):
        return remote(bmean.at[t, mine], bmean.at[t, mine], s_mean.at[t], r_mean.at[t], (partner, lat))

    def mean_wait(t):
        return remote(bmean.at[t, other], bmean.at[t, other], s_mean.at[t], r_mean.at[t], (partner, lat))

    def load_a(t):
        return pltpu.make_async_copy(raw_a.at[t], stage.at[t], c_a.at[t])

    load_v = pltpu.make_async_copy(raw_v, stage_v, c_v)
    load_u = pltpu.make_async_copy(raw_u, stage_u, c_u)
    load_v.start()

    @pl.loop(0, T)
    def _(t):
        load_a(t).start()

    load_u.start()

    barrier = pltpu.get_barrier_semaphore()
    for d in range(1, lat_n):
        pl.semaphore_signal(barrier, inc=1, device_id=(lev, (lat + d) % lat_n), device_id_type=MESH)
    for d in range(1, lev_n):
        pl.semaphore_signal(barrier, inc=1, device_id=((lev + d) % lev_n, lat), device_id_type=MESH)
    pl.semaphore_wait(barrier, lat_n + lev_n - 2)

    def tile(r, c):
        return pl.ds(c * R + r, L, stride=K)

    load_v.wait()
    for c in range(C):
        v_ref[0, c] = stage_v[tile(0, c), :]

    @pl.when(has_south)
    def _():
        v_copy().start()

    @pl.loop(0, T)
    def _(t):
        load_a(t).wait()
        staged = stage.at[t]
        for r in (0, R - 1):
            for c in range(C):
                a_ref[t, r, c] = staged[tile(r, c), :]
        halo_send(a_ref, halo0, s_h0, r_h0, t)

    slot = lax.broadcasted_iota(jnp.int32, (cap, cap), 0)
    across = lax.broadcasted_iota(jnp.int32, (cap, cap), 1)
    for d in range(lat_n):
        row = jnp.broadcast_to(column_ref[0, 0, d : d + 1, :], (cap, cap)).astype(jnp.float32) + 1.0
        used = jnp.logical_and(slot == across, slot < count_ref[0, 0, d])
        column = jnp.sum(jnp.where(used, row, 0.0), axis=1, keepdims=True)
        obs_ref[d, :, 0:levels] = values_ref[0, 0, d]
        obs_ref[d, :, levels:] = jnp.broadcast_to(column, (cap, obs_ref.shape[2] - levels))
    for d in range(1, lat_n):
        obs1(d).start()
    obs_in[0:cap] = obs_ref[lat]
    if obs_in.shape[0] > lat_n * cap:
        obs_in[lat_n * cap :] = jnp.zeros_like(obs_in[lat_n * cap :])

    @pl.loop(0, T)
    def _(t):
        staged = stage.at[t]
        for r in range(1, R - 1):
            for c in range(C):
                a_ref[t, r, c] = staged[tile(r, c), :]

    load_u.wait()
    for r in range(R):
        for c in range(C):
            u_ref[r, c] = stage_u[tile(r, c), :]
            if r > 0:
                v_ref[r, c] = stage_v[tile(r, c), :]

    block = lev * L // inv_ref.shape[3]
    for r in range(R):
        inverse = inv_ref[r, block, pl.ds(first, L), :]
        for j in range(2 * L):
            diff_ref[r, j] = jnp.broadcast_to(inverse[:, j : j + 1], (L, LANES))

    @pl.when(jnp.logical_not(has_south))
    def _():
        halo0[0] = jnp.zeros_like(halo0[0])
        halo1[0] = jnp.zeros_like(halo1[0])

    @pl.when(jnp.logical_not(has_north))
    def _():
        halo0[1] = jnp.zeros_like(halo0[1])
        halo1[1] = jnp.zeros_like(halo1[1])
        vnorth[...] = jnp.zeros_like(vnorth)

    lane = lax.broadcasted_iota(jnp.int32, (C, L, LANES), 2)

    def eastern(x):
        r = pltpu.roll(x, LANES - 1, 2)
        return jnp.where(lane == LANES - 1, jnp.concatenate([r[1:], r[:1]], axis=0), r)

    def western(x):
        r = pltpu.roll(x, 1, 2)
        return jnp.where(lane == 0, jnp.concatenate([r[-1:], r[:-1]], axis=0), r)

    level = lax.broadcasted_iota(jnp.int32, (L, LANES), 0)
    for r in range(R):
        for c in range(C):
            k = r * C + c
            lon = slice(c * LANES, (c + 1) * LANES)
            low, high = band_ref[0, r : r + 1, lon], band_ref[1, r : r + 1, lon]
            counted[k : k + 1, :] = (high - low).astype(jnp.float32)
            lo = jnp.broadcast_to(low, (L, LANES))
            hi = jnp.broadcast_to(high, (L, LANES))
            kap = jnp.broadcast_to(flux_ref[r : r + 1, lon], (L, LANES))
            for base, g in ((lev * L, go), (partner * L, gp)):
                here = jnp.where(level + base >= lo, 1.0, 0.0) * jnp.where(level + base < hi, 1.0, 0.0)
                g[r, c] = kap * here
                if g is go:
                    io[r, c] = here

    @pl.when(has_north)
    def _():
        v_copy().wait_recv()

    for r in range(R):
        u = u_ref[r]
        e = jnp.maximum(eastern(u), 0.0)
        w = jnp.minimum(u, 0.0)
        n = jnp.maximum(v_ref[r + 1] if r < R - 1 else vnorth[...], 0.0)
        s = jnp.minimum(v_ref[r], 0.0)
        fe[r], fw[r], fn[r], fs[r] = e, w, n, s
        cc[r] = 1.0 - e + w - n + s

    def substep(src, halo, dst, t):
        for r in range(R):
            x = src[t, r]
            up = src[t, r + 1] if r < R - 1 else halo[1, t]
            down = src[t, r - 1] if r > 0 else halo[0, t]
            dst[t, r] = (
                x * cc[r] + eastern(x) * fe[r] - western(x) * fw[r] + up * fn[r] - down * fs[r]
            )

    for d in range(1, lat_n):
        obs1(d).wait_recv()
    total = jnp.transpose(obs_in[...])
    for i in range(lev_n):
        msg[i, 0:L] = total[i * L : (i + 1) * L]
        msg[i, L : 2 * L] = total[levels : levels + L]
    got[lev] = msg[lev]
    for d in range(1, lev_n):
        obs2(d).start()

    @pl.loop(0, T)
    def _(t):
        halo_recv(a_ref, halo0, s_h0, r_h0, t)
        substep(a_ref, halo0, a1, t)
        halo_send(a1, halo1, s_h1, r_h1, t)

    for d in range(1, lev_n):
        obs2_wait(d).wait_recv()
    width = got.shape[2]
    diagonal = lax.broadcasted_iota(jnp.int32, (width, width), 0) == lax.broadcasted_iota(
        jnp.int32, (width, width), 1
    )

    @pl.loop(0, lev_n)
    def _(i):
        values = got[i, 0:L]
        row = got[i, L : 2 * L][0:1]
        column = jnp.sum(jnp.where(diagonal, jnp.broadcast_to(row, (width, width)), 0.0), axis=1, keepdims=True)
        column = column.astype(jnp.int32) - 1
        high = values.astype(jnp.bfloat16).astype(jnp.float32)
        rest = values - high
        middle = rest.astype(jnp.bfloat16).astype(jnp.float32)
        parts = jnp.concatenate([high, middle, rest - middle, jnp.zeros_like(high)], axis=0).astype(jnp.bfloat16)
        for c in range(tiles):
            ids = lax.broadcasted_iota(jnp.int32, (width, LANES), 1) + c * LANES
            hot = jnp.where(column == ids, 1.0, 0.0).astype(jnp.bfloat16)
            f = jnp.dot(parts, hot, preferred_element_type=jnp.float32)
            force[i * tiles + c] = f[0:L] + f[L : 2 * L] + f[2 * L : 3 * L]

    def stage_a(t):
        halo_recv(a1, halo1, s_h1, r_h1, t)
        substep(a1, halo1, a2, t)
        for r in range(R):
            ps[t, r * C : (r + 1) * C, :] = jnp.sum(a2[t, r] * io[r], axis=1)
        part(t).start()
        pair(t).start()

    def stage_b(t):
        part(t).wait_recv()
        hs[t] = ps[t, mine, :] + pr[t]
        for d in range(1, chips):
            sums(d, t).start()

    def stage_c(t):
        acc = hs[t]
        for d in range(1, chips):
            sums(d, t).wait_recv()
            acc = acc + bsr[d - 1, t]
        bmean[t, mine, :] = acc / counted[mine, :]
        mean(t).start()

    def stage_d(t):
        pair(t).wait_recv()
        mean_wait(t).wait_recv()
        finished = out_ref.at[t]
        for r in range(R):
            for c in range(C):
                k = r * C + c
                m = jnp.broadcast_to(bmean[t, k : k + 1, :], (L, LANES))
                x = a2[t, r, c]
                y = a2o[t, r, c]
                mx[r, c, pl.ds(first, L)] = x + go[r, c] * (m - x)
                mx[r, c, pl.ds(L - first, L)] = y + gp[r, c] * (m - y)
        for r in range(R):
            acc = force[r * C : (r + 1) * C]
            for j in range(2 * L):
                acc = acc + diff_ref[r, j][None] * mx[r, :, j : j + 1, :]
            for c in range(C):
                finished[tile(r, c), :] = acc[c]

    stages = (stage_a, stage_b, stage_c, stage_d)

    @pl.loop(0, T + len(stages) - 1)
    def _(s):
        for lag, run in enumerate(stages):
            @pl.when(jnp.logical_and(s >= lag, s < T + lag))
            def _():
                run(s - lag)

    for d in range(1, lat_n):
        obs1(d).wait_send()
    for d in range(1, lev_n):
        obs2(d).wait_send()

    @pl.when(has_south)
    def _():
        v_copy().wait_send()

    @pl.loop(0, T)
    def _(t):
        halo_sent(a_ref, halo0, s_h0, r_h0, t)
        halo_sent(a1, halo1, s_h1, r_h1, t)
        pair(t).wait_send()
        part(t).wait_send()
        mean(t).wait_send()
        for d in range(1, chips):
            sums(d, t).wait_send()


def body(
    adjoint_in, courant_lon, courant_lat, mass_flux, conv_band, diff_inverse,
    obs_values, obs_column, obs_count,
):
    lev_n, lat_n = lax.axis_size("lev"), lax.axis_size("lat")
    T, L, R, lon = adjoint_in.shape
    C = lon // LANES
    K = R * C
    levels, cap = obs_values.shape[-1], obs_values.shape[-2]

    a = adjoint_in.reshape(T, L, R, C, LANES).transpose(0, 1, 3, 2, 4).reshape(T, L * K, LANES)
    u = courant_lon.reshape(L, R, C, LANES).transpose(0, 2, 1, 3).reshape(L * K, LANES)
    v = courant_lat.reshape(L, R, C, LANES).transpose(0, 2, 1, 3).reshape(L * K, LANES)
    size = diff_inverse.shape[-1]
    width = -(-lat_n * cap // LANES) * LANES
    depth = -(-(levels + L) // LANES) * LANES

    chips = lev_n // 2
    f32 = jnp.float32
    vm = lambda *shape: pltpu.VMEM(shape, f32)
    dma = lambda *shape: pltpu.SemaphoreType.DMA(shape)
    scratch = [
        vm(T, L * K, LANES), vm(L * K, LANES), vm(L * K, LANES),
        vm(T, R, C, L, LANES), vm(R, C, L, LANES), vm(R, C, L, LANES),
        vm(R, size, L, LANES), vm(lat_n, cap, depth), vm(K, LANES),
        vm(T, R, C, L, LANES), vm(T, R, C, L, LANES), vm(T, R, C, L, LANES),
        vm(2, T, C, L, LANES), vm(2, T, C, L, LANES), vm(C, L, LANES),
        *[vm(R, C, L, LANES)] * 8,
        vm(R, C, 2 * L, LANES), vm(T, K, LANES), vm(T, K // 2, LANES), vm(T, K // 2, LANES),
        vm(chips - 1, T, K // 2, LANES), vm(T, K, LANES),
        vm(K, L, LANES), vm(width, depth), vm(lev_n, 2 * L, width), vm(lev_n, 2 * L, width),
        dma(T), pltpu.SemaphoreType.DMA, pltpu.SemaphoreType.DMA,
        dma(lat_n - 1), dma(lat_n - 1), dma(lev_n - 1), dma(lev_n - 1),
        pltpu.SemaphoreType.DMA, pltpu.SemaphoreType.DMA,
        dma(2, T), dma(2, T), dma(2, T), dma(2, T), dma(T), dma(T), dma(T), dma(T),
        dma(chips - 1, T), dma(chips - 1, T), dma(T), dma(T),
    ]
    vmem = pl.BlockSpec(memory_space=pltpu.VMEM)
    hbm = pl.BlockSpec(memory_space=pl.ANY)
    out = pl.pallas_call(
        functools.partial(kernel, lev_n, lat_n),
        out_shape=jax.ShapeDtypeStruct((T, L * K, LANES), f32),
        in_specs=[hbm] * 3 + [vmem] * 5 + [pl.BlockSpec(memory_space=pltpu.SMEM)],
        out_specs=pl.BlockSpec(memory_space=pltpu.VMEM),
        scratch_shapes=scratch,
        compiler_params=pltpu.CompilerParams(
            collective_id=0, has_side_effects=True, vmem_limit_bytes=44 * 1024 * 1024
        ),
    )(a, u, v, conv_band, mass_flux, diff_inverse, obs_values, obs_column, obs_count)
    return out.reshape(T, L, C, R, LANES).transpose(0, 1, 3, 2, 4).reshape(T, L, R, lon)


def solution(mesh):
    placed = (
        P(None, "lev", "lat", None),
        P("lev", "lat", None),
        P("lev", "lat", None),
        P("lat", None),
        P(None, "lat", None),
        P("lat", None, None, None),
        P("lev", "lat", None, None, None),
        P("lev", "lat", None, None),
        P("lev", "lat", None),
    )
    return jax.shard_map(
        body, mesh=mesh, in_specs=placed, out_specs=P(None, "lev", "lat", None), check_vma=False
    )
```

```python
import functools

import jax
import jax.numpy as jnp
from jax import lax
from jax.experimental import pallas as pl
from jax.experimental.pallas import tpu as pltpu
from jax.sharding import PartitionSpec as P

MESH = pl.DeviceIdType.MESH
LANES = 128


def kernel(
    lev_n, lat_n,
    raw_a, raw_u, raw_v, raw_band, raw_flux, raw_inv, raw_values, raw_column, raw_count,
    out_ref,
    band_ref, flux_ref, inv_ref, values_ref, column_ref, count_ref,
    stage, stage_u, stage_v, a_ref, u_ref, v_ref, diff_ref, obs_ref, counted,
    a1, a2, a2o, halo0, halo1, vnorth, cc, fe, fw, fn, fs,
    io, go, gp, mx, ps, pr, hs, bsr, bmean, force, obs_in, msg, got,
    c_small, c_a, c_u, c_v, s_obs1, r_obs1, s_obs2, r_obs2, s_v, r_v, s_h0, r_h0, s_h1, r_h1, s_pair, r_pair,
    s_part, r_part, s_bs, r_bs, s_mean, r_mean,
):
    T, R, C, L, _ = a_ref.shape
    K = R * C
    H = K // 2
    half = lax.axis_index("lev") % 2
    lev = lax.axis_index("lev")
    lat = lax.axis_index("lat")
    chips = lev_n // 2
    partner = lev + 1 - 2 * (lev % 2)
    has_north = lat < lat_n - 1
    has_south = lat > 0
    tiles = R * C // lev_n
    levels = lev_n * L
    cap = values_ref.shape[3]
    first = pl.multiple_of(half * L, L)
    mine = pl.ds(pl.multiple_of(half * H, H), H)
    other = pl.ds(pl.multiple_of((1 - half) * H, H), H)

    def remote(src, dst, s, r, dev):
        return pltpu.make_async_remote_copy(
            src_ref=src, dst_ref=dst, send_sem=s, recv_sem=r, device_id=dev, device_id_type=MESH
        )

    def obs1(d):
        to = (lat + d) % lat_n
        return remote(obs_ref.at[to], obs_in.at[pl.ds(d * cap, cap)], s_obs1.at[d - 1], r_obs1.at[d - 1], (lev, to))

    def obs2(d):
        to = (lev + d) % lev_n
        return remote(msg.at[to], got.at[lev], s_obs2.at[d - 1], r_obs2.at[d - 1], (to, lat))

    def obs2_wait(d):
        src = (lev - d + lev_n) % lev_n
        return remote(msg.at[src], got.at[src], s_obs2.at[d - 1], r_obs2.at[d - 1], (src, lat))

    def south(src, dst, s, r):
        return remote(src, dst, s, r, (lev, lax.max(lat - 1, 0)))

    def north(src, dst, s, r):
        return remote(src, dst, s, r, (lev, lax.min(lat + 1, lat_n - 1)))

    def v_copy():
        return south(v_ref.at[0], vnorth, s_v, r_v)

    def halo_south(src, dst, s, r, t):
        return south(src.at[t, 0], dst.at[1, t], s.at[1, t], r.at[1, t])

    def halo_north(src, dst, s, r, t):
        return north(src.at[t, R - 1], dst.at[0, t], s.at[0, t], r.at[0, t])

    def halo_send(src, dst, s, r, t):
        @pl.when(has_south)
        def _():
            halo_south(src, dst, s, r, t).start()

        @pl.when(has_north)
        def _():
            halo_north(src, dst, s, r, t).start()

    def halo_recv(src, dst, s, r, t):
        @pl.when(has_south)
        def _():
            halo_north(src, dst, s, r, t).wait_recv()

        @pl.when(has_north)
        def _():
            halo_south(src, dst, s, r, t).wait_recv()

    def halo_sent(src, dst, s, r, t):
        @pl.when(has_south)
        def _():
            halo_south(src, dst, s, r, t).wait_send()

        @pl.when(has_north)
        def _():
            halo_north(src, dst, s, r, t).wait_send()

    def pair(t):
        return remote(a2.at[t], a2o.at[t], s_pair.at[t], r_pair.at[t], (partner, lat))

    def part(t):
        return remote(ps.at[t, other], pr.at[t], s_part.at[t], r_part.at[t], (partner, lat))

    def sums(d, t):
        to = (lev + 2 * d) % lev_n
        return remote(hs.at[t], bsr.at[d - 1, t], s_bs.at[d - 1, t], r_bs.at[d - 1, t], (to, lat))

    def mean(t):
        return remote(bmean.at[t, mine], bmean.at[t, mine], s_mean.at[t], r_mean.at[t], (partner, lat))

    def mean_wait(t):
        return remote(bmean.at[t, other], bmean.at[t, other], s_mean.at[t], r_mean.at[t], (partner, lat))

    def load_a(t):
        return pltpu.make_async_copy(raw_a.at[t], stage.at[t], c_a.at[t])

    load_v = pltpu.make_async_copy(raw_v, stage_v, c_v)
    load_u = pltpu.make_async_copy(raw_u, stage_u, c_u)
    load_v.start()

    @pl.loop(0, T)
    def _(t):
        load_a(t).start()

    load_u.start()
    small = [
        pltpu.make_async_copy(src, dst, c_small.at[i])
        for i, (src, dst) in enumerate((
            (raw_values, values_ref), (raw_column, column_ref), (raw_count, count_ref),
            (raw_inv, inv_ref), (raw_band, band_ref), (raw_flux, flux_ref),
        ))
    ]
    for load in small:
        load.start()

    barrier = pltpu.get_barrier_semaphore()
    for d in range(1, lat_n):
        pl.semaphore_signal(barrier, inc=1, device_id=(lev, (lat + d) % lat_n), device_id_type=MESH)
    for d in range(1, lev_n):
        pl.semaphore_signal(barrier, inc=1, device_id=((lev + d) % lev_n, lat), device_id_type=MESH)
    pl.semaphore_wait(barrier, lat_n + lev_n - 2)

    def tile(r, c):
        return pl.ds(c * R + r, L, stride=K)

    load_v.wait()
    for c in range(C):
        v_ref[0, c] = stage_v[tile(0, c), :]

    @pl.when(has_south)
    def _():
        v_copy().start()

    @pl.loop(0, T)
    def _(t):
        load_a(t).wait()
        staged = stage.at[t]
        for r in (0, R - 1):
            for c in range(C):
                a_ref[t, r, c] = staged[tile(r, c), :]
        halo_send(a_ref, halo0, s_h0, r_h0, t)

    for load in small:
        load.wait()

    slot = lax.broadcasted_iota(jnp.int32, (cap, cap), 0)
    across = lax.broadcasted_iota(jnp.int32, (cap, cap), 1)
    for d in range(lat_n):
        row = jnp.broadcast_to(column_ref[0, 0, d : d + 1, :], (cap, cap)).astype(jnp.float32) + 1.0
        used = jnp.logical_and(slot == across, slot < count_ref[0, 0, d])
        column = jnp.sum(jnp.where(used, row, 0.0), axis=1, keepdims=True)
        obs_ref[d, :, 0:levels] = values_ref[0, 0, d]
        obs_ref[d, :, levels:] = jnp.broadcast_to(column, (cap, obs_ref.shape[2] - levels))
    for d in range(1, lat_n):
        obs1(d).start()
    obs_in[0:cap] = obs_ref[lat]
    if obs_in.shape[0] > lat_n * cap:
        obs_in[lat_n * cap :] = jnp.zeros_like(obs_in[lat_n * cap :])

    @pl.loop(0, T)
    def _(t):
        staged = stage.at[t]
        for r in range(1, R - 1):
            for c in range(C):
                a_ref[t, r, c] = staged[tile(r, c), :]

    load_u.wait()
    for r in range(R):
        for c in range(C):
            u_ref[r, c] = stage_u[tile(r, c), :]
            if r > 0:
                v_ref[r, c] = stage_v[tile(r, c), :]

    block = lev * L // inv_ref.shape[3]
    for r in range(R):
        inverse = inv_ref[r, block, pl.ds(first, L), :]
        for j in range(2 * L):
            diff_ref[r, j] = jnp.broadcast_to(inverse[:, j : j + 1], (L, LANES))

    @pl.when(jnp.logical_not(has_south))
    def _():
        halo0[0] = jnp.zeros_like(halo0[0])
        halo1[0] = jnp.zeros_like(halo1[0])

    @pl.when(jnp.logical_not(has_north))
    def _():
        halo0[1] = jnp.zeros_like(halo0[1])
        halo1[1] = jnp.zeros_like(halo1[1])
        vnorth[...] = jnp.zeros_like(vnorth)

    lane = lax.broadcasted_iota(jnp.int32, (C, L, LANES), 2)

    def eastern(x):
        r = pltpu.roll(x, LANES - 1, 2)
        return jnp.where(lane == LANES - 1, jnp.concatenate([r[1:], r[:1]], axis=0), r)

    def western(x):
        r = pltpu.roll(x, 1, 2)
        return jnp.where(lane == 0, jnp.concatenate([r[-1:], r[:-1]], axis=0), r)

    level = lax.broadcasted_iota(jnp.int32, (L, LANES), 0)
    for r in range(R):
        for c in range(C):
            k = r * C + c
            lon = slice(c * LANES, (c + 1) * LANES)
            low, high = band_ref[0, r : r + 1, lon], band_ref[1, r : r + 1, lon]
            counted[k : k + 1, :] = (high - low).astype(jnp.float32)
            lo = jnp.broadcast_to(low, (L, LANES))
            hi = jnp.broadcast_to(high, (L, LANES))
            kap = jnp.broadcast_to(flux_ref[r : r + 1, lon], (L, LANES))
            for base, g in ((lev * L, go), (partner * L, gp)):
                here = jnp.where(level + base >= lo, 1.0, 0.0) * jnp.where(level + base < hi, 1.0, 0.0)
                g[r, c] = kap * here
                if g is go:
                    io[r, c] = here

    @pl.when(has_north)
    def _():
        v_copy().wait_recv()

    for r in range(R):
        u = u_ref[r]
        e = jnp.maximum(eastern(u), 0.0)
        w = jnp.minimum(u, 0.0)
        n = jnp.maximum(v_ref[r + 1] if r < R - 1 else vnorth[...], 0.0)
        s = jnp.minimum(v_ref[r], 0.0)
        fe[r], fw[r], fn[r], fs[r] = e, w, n, s
        cc[r] = 1.0 - e + w - n + s

    def substep(src, halo, dst, t):
        for r in range(R):
            x = src[t, r]
            up = src[t, r + 1] if r < R - 1 else halo[1, t]
            down = src[t, r - 1] if r > 0 else halo[0, t]
            dst[t, r] = (
                x * cc[r] + eastern(x) * fe[r] - western(x) * fw[r] + up * fn[r] - down * fs[r]
            )

    for d in range(1, lat_n):
        obs1(d).wait_recv()
    total = jnp.transpose(obs_in[...])
    for i in range(lev_n):
        msg[i, 0:L] = total[i * L : (i + 1) * L]
        msg[i, L : 2 * L] = total[levels : levels + L]
    got[lev] = msg[lev]
    for d in range(1, lev_n):
        obs2(d).start()

    @pl.loop(0, T)
    def _(t):
        halo_recv(a_ref, halo0, s_h0, r_h0, t)
        substep(a_ref, halo0, a1, t)
        halo_send(a1, halo1, s_h1, r_h1, t)

    for d in range(1, lev_n):
        obs2_wait(d).wait_recv()
    width = got.shape[2]
    diagonal = lax.broadcasted_iota(jnp.int32, (width, width), 0) == lax.broadcasted_iota(
        jnp.int32, (width, width), 1
    )

    @pl.loop(0, lev_n)
    def _(i):
        values = got[i, 0:L]
        row = got[i, L : 2 * L][0:1]
        column = jnp.sum(jnp.where(diagonal, jnp.broadcast_to(row, (width, width)), 0.0), axis=1, keepdims=True)
        column = column.astype(jnp.int32) - 1
        high = values.astype(jnp.bfloat16).astype(jnp.float32)
        rest = values - high
        middle = rest.astype(jnp.bfloat16).astype(jnp.float32)
        parts = jnp.concatenate([high, middle, rest - middle, jnp.zeros_like(high)], axis=0).astype(jnp.bfloat16)
        for c in range(tiles):
            ids = lax.broadcasted_iota(jnp.int32, (width, LANES), 1) + c * LANES
            hot = jnp.where(column == ids, 1.0, 0.0).astype(jnp.bfloat16)
            f = jnp.dot(parts, hot, preferred_element_type=jnp.float32)
            force[i * tiles + c] = f[0:L] + f[L : 2 * L] + f[2 * L : 3 * L]

    def stage_a(t):
        halo_recv(a1, halo1, s_h1, r_h1, t)
        substep(a1, halo1, a2, t)
        for r in range(R):
            ps[t, r * C : (r + 1) * C, :] = jnp.sum(a2[t, r] * io[r], axis=1)
        part(t).start()
        pair(t).start()

    def stage_b(t):
        part(t).wait_recv()
        hs[t] = ps[t, mine, :] + pr[t]
        for d in range(1, chips):
            sums(d, t).start()

    def stage_c(t):
        acc = hs[t]
        for d in range(1, chips):
            sums(d, t).wait_recv()
            acc = acc + bsr[d - 1, t]
        bmean[t, mine, :] = acc / counted[mine, :]
        mean(t).start()

    def stage_d(t):
        pair(t).wait_recv()
        mean_wait(t).wait_recv()
        finished = out_ref.at[t]
        for r in range(R):
            for c in range(C):
                k = r * C + c
                m = jnp.broadcast_to(bmean[t, k : k + 1, :], (L, LANES))
                x = a2[t, r, c]
                y = a2o[t, r, c]
                mx[r, c, pl.ds(first, L)] = x + go[r, c] * (m - x)
                mx[r, c, pl.ds(L - first, L)] = y + gp[r, c] * (m - y)
        for r in range(R):
            acc = force[r * C : (r + 1) * C]
            for j in range(2 * L):
                acc = acc + diff_ref[r, j][None] * mx[r, :, j : j + 1, :]
            for c in range(C):
                finished[tile(r, c), :] = acc[c]

    stages = ((stage_d, 7), (stage_c, 5), (stage_b, 2), (stage_a, 0))

    @pl.loop(0, T + 7)
    def _(s):
        for run, lag in stages:
            @pl.when(jnp.logical_and(s >= lag, s < T + lag))
            def _():
                run(s - lag)

    for d in range(1, lat_n):
        obs1(d).wait_send()
    for d in range(1, lev_n):
        obs2(d).wait_send()

    @pl.when(has_south)
    def _():
        v_copy().wait_send()

    @pl.loop(0, T)
    def _(t):
        halo_sent(a_ref, halo0, s_h0, r_h0, t)
        halo_sent(a1, halo1, s_h1, r_h1, t)
        pair(t).wait_send()
        part(t).wait_send()
        mean(t).wait_send()
        for d in range(1, chips):
            sums(d, t).wait_send()


def body(
    adjoint_in, courant_lon, courant_lat, mass_flux, conv_band, diff_inverse,
    obs_values, obs_column, obs_count,
):
    lev_n, lat_n = lax.axis_size("lev"), lax.axis_size("lat")
    T, L, R, lon = adjoint_in.shape
    C = lon // LANES
    K = R * C
    levels, cap = obs_values.shape[-1], obs_values.shape[-2]

    a = adjoint_in.reshape(T, L, R, C, LANES).transpose(0, 1, 3, 2, 4).reshape(T, L * K, LANES)
    u = courant_lon.reshape(L, R, C, LANES).transpose(0, 2, 1, 3).reshape(L * K, LANES)
    v = courant_lat.reshape(L, R, C, LANES).transpose(0, 2, 1, 3).reshape(L * K, LANES)
    size = diff_inverse.shape[-1]
    width = -(-lat_n * cap // LANES) * LANES
    depth = -(-(levels + L) // LANES) * LANES

    chips = lev_n // 2
    f32 = jnp.float32
    vm = lambda *shape: pltpu.VMEM(shape, f32)
    dma = lambda *shape: pltpu.SemaphoreType.DMA(shape)
    operands = (conv_band, mass_flux, diff_inverse, obs_values, obs_column)
    scratch = [
        *[pltpu.VMEM(x.shape, x.dtype) for x in operands], pltpu.SMEM(obs_count.shape, obs_count.dtype),
        vm(T, L * K, LANES), vm(L * K, LANES), vm(L * K, LANES),
        vm(T, R, C, L, LANES), vm(R, C, L, LANES), vm(R, C, L, LANES),
        vm(R, size, L, LANES), vm(lat_n, cap, depth), vm(K, LANES),
        vm(T, R, C, L, LANES), vm(T, R, C, L, LANES), vm(T, R, C, L, LANES),
        vm(2, T, C, L, LANES), vm(2, T, C, L, LANES), vm(C, L, LANES),
        *[vm(R, C, L, LANES)] * 8,
        vm(R, C, 2 * L, LANES), vm(T, K, LANES), vm(T, K // 2, LANES), vm(T, K // 2, LANES),
        vm(chips - 1, T, K // 2, LANES), vm(T, K, LANES),
        vm(K, L, LANES), vm(width, depth), vm(lev_n, 2 * L, width), vm(lev_n, 2 * L, width),
        dma(6), dma(T), pltpu.SemaphoreType.DMA, pltpu.SemaphoreType.DMA,
        dma(lat_n - 1), dma(lat_n - 1), dma(lev_n - 1), dma(lev_n - 1),
        pltpu.SemaphoreType.DMA, pltpu.SemaphoreType.DMA,
        dma(2, T), dma(2, T), dma(2, T), dma(2, T), dma(T), dma(T), dma(T), dma(T),
        dma(chips - 1, T), dma(chips - 1, T), dma(T), dma(T),
    ]
    vmem = pl.BlockSpec(memory_space=pltpu.VMEM)
    hbm = pl.BlockSpec(memory_space=pltpu.HBM)
    out = pl.pallas_call(
        functools.partial(kernel, lev_n, lat_n),
        out_shape=jax.ShapeDtypeStruct((T, L * K, LANES), f32),
        in_specs=[hbm] * 9,
        out_specs=vmem,
        scratch_shapes=scratch,
        compiler_params=pltpu.CompilerParams(
            collective_id=0, has_side_effects=True, vmem_limit_bytes=63 * 1024 * 1024
        ),
    )(a, u, v, conv_band, mass_flux, diff_inverse, obs_values, obs_column, obs_count)
    return out.reshape(T, L, C, R, LANES).transpose(0, 1, 3, 2, 4).reshape(T, L, R, lon)


def solution(mesh):
    placed = (
        P(None, "lev", "lat", None),
        P("lev", "lat", None),
        P("lev", "lat", None),
        P("lat", None),
        P(None, "lat", None),
        P("lat", None, None, None),
        P("lev", "lat", None, None, None),
        P("lev", "lat", None, None),
        P("lev", "lat", None),
    )
    return jax.shard_map(
        body, mesh=mesh, in_specs=placed, out_specs=P(None, "lev", "lat", None), check_vma=False
    )
```
